32 devices in a mesh: row: 4 (over y, x), col: 2 (over core), depth: 4 (over z).
Axes of the slice: x: 2, y: 2, z: 4, core: 2. Of those that a mesh axis runs over, the one named last changes fastest.
Arguments:
- left_slab: bfloat16 [4096, 4096], P(None, ('col', 'depth')), may hold values from -6 to 6
- right_vectors: bfloat16 [65536, 4096], P('col', 'depth'), may hold values from -0.09375 to 0.09375
- pair_weight: float32 [4096], P(('col', 'depth')), may hold values from -6 to 6
- eigenvalue: float32 [4096], P(('col', 'depth')), may hold values from -2 to 2
- pair_order: int32 [4096], replicated, may hold values from 0 to 4095, each once
- row_offset: int32 [1], replicated, may hold values from 0 to 3072
Outputs:
- grads: bfloat16 [3, 1024, 65536], P(None, 'row', ('col', 'depth'))
The draws below stay inside these ranges and needn't reach their ends.
Inputs may be any that keep to these rules, and one draw needn't show every extreme that they name: `pair_order`: each of 0 to 4095 appears exactly once.
All inputs are finite; a program needn't handle non-finite values.
Results may differ from the reference program's by a relative error of at most 0.023.
Values may be sent and summed in bfloat16 or wider, within the bound.
A program may use at most 192 MiB of HBM per device.

```python
import jax
import jax.numpy as jnp
from jax import lax

N = 65536
K = 4096
P_SIZE = 1024
SLAB = 4096
N_COL = 2
N_DEPTH = 4


def block_scale(rng, dims, shards, smallest, largest):
    gain, own = 1.0, jax.random.fold_in(rng, 6)
    for axis_at, blocks in shards:
        draws = jnp.exp(jax.random.uniform(jax.random.fold_in(own, axis_at), (blocks,), jnp.float32, smallest / len(shards), largest / len(shards)))
        gain = gain * jnp.repeat(draws, dims[axis_at] // blocks).reshape([-1 if axis == axis_at else 1 for axis in range(len(dims))])
    return gain


def centred(own_key, shape, spread, bound, shards=(), kind=jnp.bfloat16):
    loudness = block_scale(own_key, shape, shards, -0.22, 0.18) if shards else 1.0
    values = jax.random.normal(own_key, shape, jnp.float32) * spread * loudness
    return jnp.minimum(jnp.maximum(values, -bound), bound).astype(kind)


def setup_inputs(seed: int = 0) -> dict:
    arg_keys = jax.random.split(jax.random.key(seed), 7)
    left_slab = centred(arg_keys[0], (SLAB, K), 1.0, 6.0, ((1, 8),))
    right_vectors = centred(arg_keys[1], (N, K), K ** -0.5, 0.09375, ((0, 2), (1, 4)))
    pair_weight = centred(arg_keys[2], (K,), 1.0, 6.0, ((0, 8),), jnp.float32)
    eigenvalue = jnp.clip(jax.random.uniform(arg_keys[3], (K,), jnp.float32, -2.0, 2.0) * block_scale(arg_keys[3], (K,), ((0, 8),), -0.4, 0.0), -2.0, 2.0)
    pair_order = jax.random.permutation(arg_keys[4], K).astype(jnp.int32)
    row_offset = jax.random.randint(arg_keys[5], (1,), 0, SLAB - P_SIZE + 1).astype(jnp.int32)
    return dict(left_slab=left_slab, right_vectors=right_vectors, pair_weight=pair_weight, eigenvalue=eigenvalue, pair_order=pair_order, row_offset=row_offset)


def reference(left_slab, right_vectors, pair_weight, eigenvalue, pair_order, row_offset):
    panel = lax.dynamic_slice_in_dim(left_slab, row_offset[0].astype(jnp.int32), P_SIZE, 0)
    ordered = panel[:, pair_order].astype(jnp.float32)
    weight = pair_weight[pair_order]
    lam = eigenvalue[pair_order]
    powers = jnp.stack([weight, weight * lam, weight * lam * lam])
    scaled = (ordered[None, :, :] * powers[:, None, :]).astype(jnp.bfloat16).reshape(3 * P_SIZE, K)
    group_width = K // N_DEPTH
    block_cols = N // N_COL

    def column_block(index):
        start = (index * block_cols).astype(jnp.int32)
        columns = lax.dynamic_slice_in_dim(right_vectors, start, block_cols, 0)
        total = jnp.zeros((3 * P_SIZE, block_cols), jnp.float32)
        for group in range(N_DEPTH):
            lo = group * group_width
            part = lax.dot_general(scaled[:, lo:lo + group_width], columns[:, lo:lo + group_width],
                                   (((1,), (1,)), ((), ())), preferred_element_type=jnp.float32)
            total = total + part.astype(jnp.bfloat16).astype(jnp.float32)
        return total.astype(jnp.bfloat16)

    blocks = lax.map(column_block, jnp.arange(N_COL, dtype=jnp.int32))
    blocks = blocks.reshape(N_COL, 3, P_SIZE, block_cols)
    return jnp.transpose(blocks, (1, 2, 0, 3)).reshape(3, P_SIZE, N)
```

```python
import jax
import jax.numpy as jnp
from jax import lax
from jax.sharding import PartitionSpec as P

P_SIZE = 1024
SCALARS = 16


def split_widths(width):
    if width % 2048 == 0:
        unit = width // 16
        return [4 * unit, 4 * unit, 4 * unit, 2 * unit, 2 * unit]
    return [width]


def two_halves(values):
    high = values.astype(jnp.bfloat16)
    low = (values - high.astype(jnp.float32)).astype(jnp.bfloat16)
    return [high, low]


def gather_panel(left_slab, pair_weight, eigenvalue, members, row_offset):
    rows = P_SIZE // lax.axis_size("row")
    start = row_offset[0] + lax.axis_index("row") * rows
    mine = lax.dynamic_slice_in_dim(left_slab, start, rows, 0)
    scalars = jnp.stack(two_halves(pair_weight) + two_halves(eigenvalue))
    scalars = jnp.pad(scalars, ((0, SCALARS - scalars.shape[0]), (0, 0)))
    block = jnp.concatenate([mine, scalars], axis=0)
    block = lax.all_gather(block, ("col", "depth"), axis=1, tiled=True)
    block = jnp.take(block, members, axis=1)
    scalars = block[rows:].astype(jnp.float32)
    weight = scalars[0] + scalars[1]
    lam = scalars[2] + scalars[3]
    panel = lax.all_gather(block[:rows], "row", axis=0, tiled=False)
    powers = jnp.stack([weight, weight * lam, weight * lam * lam])
    scaled = panel.astype(jnp.float32)[:, None] * powers[None, :, None, :]
    return scaled.astype(jnp.bfloat16).reshape(3 * P_SIZE, members.shape[0])


def on_device(left_slab, right_vectors, pair_weight, eigenvalue, pair_order, row_offset):
    n_row, n_depth = lax.axis_size("row"), lax.axis_size("depth")
    row, depth = lax.axis_index("row"), lax.axis_index("depth")
    group = right_vectors.shape[1]
    owned = right_vectors.shape[0] // n_depth
    quarter = owned // n_row
    rows = P_SIZE // n_row

    sources = lax.rem(depth - jnp.arange(n_depth, dtype=jnp.int32) + n_depth, n_depth)
    members = jnp.take(pair_order.reshape(n_depth, group), sources, axis=0).reshape(-1)

    widths = split_widths(quarter)
    offsets = [sum(widths[:j]) for j in range(len(widths))]
    received = []
    for j, (offset, width) in enumerate(zip(offsets, widths)):
        pieces = []
        for step in range(n_depth):
            target = lax.rem(depth + step, n_depth)
            begin = target * owned + row * quarter + offset
            pieces.append(lax.dynamic_slice(right_vectors, (begin, 0), (width, group)))
        if j >= 2:
            tied = lax.optimization_barrier((pieces[1:], received[j - 2]))
            pieces[1:], received[j - 2] = tied
        for step in range(1, n_depth):
            pieces[step] = lax.ppermute(
                pieces[step], "depth", [(i, (i + step) % n_depth) for i in range(n_depth)]
            )
        received.append(pieces)

    scaled = gather_panel(left_slab, pair_weight, eigenvalue, members, row_offset)

    total = jnp.zeros((3, rows, owned), jnp.bfloat16)
    for offset, width, pieces in zip(offsets, widths, received):
        columns = jnp.concatenate(pieces, axis=1)
        part = lax.dot_general(
            scaled, columns, (((1,), (1,)), ((), ())), preferred_element_type=jnp.float32
        ).astype(jnp.bfloat16)
        part = part.reshape(n_row, 3, rows, width)
        for step in range(n_row):
            other = row ^ step
            piece = lax.dynamic_index_in_dim(part, other, 0, keepdims=False)
            if step:
                piece = lax.ppermute(piece, "row", [(i, i ^ step) for i in range(n_row)])
            total = lax.dynamic_update_slice(total, piece, (0, 0, other * quarter + offset))
    return total


def solution(mesh):
    in_specs = (
        P(None, ("col", "depth")),
        P("col", "depth"),
        P(("col", "depth")),
        P(("col", "depth")),
        P(),
        P(),
    )
    out_specs = P(None, "row", ("col", "depth"))
    return jax.shard_map(
        on_device, mesh=mesh, in_specs=in_specs, out_specs=out_specs, check_vma=False
    )
```

```python
import jax
import jax.numpy as jnp
from jax import lax
from jax.sharding import PartitionSpec as P

P_SIZE = 1024
SCALARS = 16


def split_widths(width):
    if width % 2048 == 0:
        unit = width // 16
        return [unit, 3 * unit, 5 * unit, 4 * unit, 3 * unit]
    return [width]


def after(values, *earlier):
    return lax.optimization_barrier((values, earlier))[0]


def two_halves(values):
    high = values.astype(jnp.bfloat16)
    low = (values - high.astype(jnp.float32)).astype(jnp.bfloat16)
    return [high, low]


def gather_panel(left_slab, pair_weight, eigenvalue, members, row_offset, arrived):
    rows = P_SIZE // lax.axis_size("row")
    start = row_offset[0] + lax.axis_index("row") * rows
    mine = lax.dynamic_slice_in_dim(left_slab, start, rows, 0)
    scalars = jnp.stack(two_halves(pair_weight) + two_halves(eigenvalue))
    scalars = jnp.pad(scalars, ((0, SCALARS - scalars.shape[0]), (0, 0)))
    block = jnp.concatenate([mine, scalars], axis=0)
    block = after(block, arrived[0])
    block = lax.all_gather(block, ("col", "depth"), axis=1, tiled=True)
    block = jnp.take(block, members, axis=1)
    scalars = block[rows:].astype(jnp.float32)
    weight = scalars[0] + scalars[1]
    lam = scalars[2] + scalars[3]
    panel = block[:rows]
    if len(arrived) > 1:
        panel = after(panel, arrived[1])
    panel = lax.all_gather(panel, "row", axis=0, tiled=False)
    if len(arrived) > 2:
        panel = after(panel, arrived[2])
    powers = jnp.stack([weight, weight * lam, weight * lam * lam])
    scaled = panel.astype(jnp.float32)[:, None] * powers[None, :, None, :]
    return scaled.astype(jnp.bfloat16).reshape(3 * P_SIZE, members.shape[0])


def on_device(left_slab, right_vectors, pair_weight, eigenvalue, pair_order, row_offset):
    n_row, n_depth = lax.axis_size("row"), lax.axis_size("depth")
    row, depth = lax.axis_index("row"), lax.axis_index("depth")
    group = right_vectors.shape[1]
    owned = right_vectors.shape[0] // n_depth
    quarter = owned // n_row
    rows = P_SIZE // n_row

    sources = lax.rem(depth - jnp.arange(n_depth, dtype=jnp.int32) + n_depth, n_depth)
    members = jnp.take(pair_order.reshape(n_depth, group), sources, axis=0).reshape(-1)

    widths = split_widths(quarter)
    offsets = [sum(widths[:j]) for j in range(len(widths))]
    starts = [
        lax.rem(depth + step, n_depth) * owned + row * quarter for step in range(n_depth)
    ]
    received = []
    products = []
    landed = []
    scaled = None

    def fetch(j):
        pieces = [
            lax.dynamic_slice(right_vectors, (begin + offsets[j], 0), (widths[j], group))
            for begin in starts
        ]
        if j >= 2:
            pieces[1:] = after(pieces[1:], received[j - 2][1:])
        if j >= 4:
            pieces[1:] = after(pieces[1:], products[j - 4])
        for step in range(1, n_depth):
            pieces[step] = lax.ppermute(
                pieces[step], "depth", [(i, (i + step) % n_depth) for i in range(n_depth)]
            )
        received.append(pieces)

    def multiply(j):
        pieces = received[j]
        if j >= 1:
            pieces = after(pieces, products[j - 1])
        if j >= 4:
            pieces = after(pieces, landed[j - 2])
        columns = jnp.concatenate(pieces, axis=1)
        part = lax.dot_general(
            scaled, columns, (((1,), (1,)), ((), ())), preferred_element_type=jnp.float32
        ).astype(jnp.bfloat16)
        part = part.reshape(n_row, 3, rows, widths[j])
        products.append(part)
        blocks = []
        for step in range(n_row):
            piece = lax.dynamic_index_in_dim(part, row ^ step, 0, keepdims=False)
            if step:
                piece = lax.ppermute(piece, "row", [(i, i ^ step) for i in range(n_row)])
            blocks.append(piece)
        landed.append(blocks)

    count = len(widths)
    for j in range(min(count, 4)):
        fetch(j)
    scaled = gather_panel(
        left_slab, pair_weight, eigenvalue, members, row_offset, [p[1:] for p in received[:3]]
    )
    for j in range(count):
        multiply(j)
        if j + 4 < count:
            fetch(j + 4)

    total = jnp.zeros((3, rows, owned), jnp.bfloat16)
    for offset, blocks in zip(offsets, landed):
        for step, piece in enumerate(blocks):
            begin = (row ^ step) * quarter + offset
            total = lax.dynamic_update_slice(total, piece, (0, 0, begin))
    return total


def solution(mesh):
    in_specs = (
        P(None, ("col", "depth")),
        P("col", "depth"),
        P(("col", "depth")),
        P(("col", "depth")),
        P(),
        P(),
    )
    out_specs = P(None, "row", ("col", "depth"))
    return jax.shard_map(
        on_device, mesh=mesh, in_specs=in_specs, out_specs=out_specs, check_vma=False
    )
```
